256 devices in a mesh: row: 32 (over y, x, core), col: 8 (over z).
Axes of the slice: x: 4, y: 4, z: 8, core: 2. Of those that a mesh axis runs over, the one named last changes fastest.
Arguments:
- tokens: bfloat16 [768, 8192], P('row', 'col'), may hold values from -6 to 6
- cotangent: bfloat16 [768, 8192], P('row', 'col'), may hold values from -1.5 to 1.5
- gate_weight: bfloat16 [8192, 28672], P('col', 'row'), may hold values from -0.0625 to 0.0625
- up_weight: bfloat16 [8192, 28672], P('col', 'row'), may hold values from -0.0625 to 0.0625
- down_weight: bfloat16 [28672, 8192], P('row', 'col'), may hold values from -0.03125 to 0.03125
Outputs:
- mixed: bfloat16 [768, 8192], P('row', 'col')
- grad_tokens: bfloat16 [768, 8192], P('row', 'col')
- grad_gate: bfloat16 [8192, 28672], P('col', 'row')
- grad_up: bfloat16 [8192, 28672], P('col', 'row')
- grad_down: bfloat16 [28672, 8192], P('row', 'col')
The draws below stay inside these ranges and needn't reach their ends.
All inputs are finite; a program needn't handle non-finite values.
Results may differ from the reference program's by a relative error of at most 0.005.
Values may be sent and summed in bfloat16 or wider, within the bound.
No kernel may reach another device: no remote copies, remote signals or barrier semaphores. Data moves between devices by JAX's collectives and lax.ppermute only.
A program may use at most 128 MiB of HBM per device.

```python
import jax
import jax.numpy as jnp

D = 8192
FF = 28672
TOKENS = 768


def level_of(stream_key, shape, shards, smallest, top_value):
    def one(position, parts):
        heights = jax.random.uniform(jax.random.fold_in(jax.random.fold_in(stream_key, 6), position), (parts,), jnp.float32, smallest / len(shards), top_value / len(shards))
        return jnp.repeat(jnp.exp(heights), shape[position] // parts).reshape((-1,) + (1,) * (len(shape) - position - 1))

    level = one(*shards[0])
    for cut in shards[1:]:
        level = level * one(*cut)
    return level


def noise(key, extent, scale, bound, cuts=(), dtype=jnp.bfloat16):
    level = level_of(key, extent, cuts, -0.22, 0.18) if cuts else 1.0
    entries = jax.random.normal(key, extent, jnp.float32) * scale * level
    return jnp.minimum(jnp.maximum(entries, -bound), bound).astype(dtype)


def setup_inputs(seed: int = 0) -> dict:
    keys = jax.random.split(jax.random.key(seed), 6)
    tokens = noise(keys[0], (TOKENS, D), 1.0, 6.0, ((0, 32), (1, 8)))
    cotangent = noise(keys[1], (TOKENS, D), 0.25, 1.5, ((0, 32), (1, 8)))
    gate_weight = noise(keys[2], (D, FF), D ** -0.5, 0.0625, ((0, 8), (1, 32)))
    up_weight = noise(keys[3], (D, FF), D ** -0.5, 0.0625, ((0, 8), (1, 32)))
    down_weight = noise(keys[4], (FF, D), FF ** -0.5, 0.03125, ((0, 32), (1, 8)))
    return dict(tokens=tokens, cotangent=cotangent, gate_weight=gate_weight, up_weight=up_weight, down_weight=down_weight)


def reference(tokens, cotangent, gate_weight, up_weight, down_weight):
    gate_proj = jnp.dot(tokens, gate_weight, preferred_element_type=jnp.float32)
    up_proj = jnp.dot(tokens, up_weight, preferred_element_type=jnp.float32)
    sigmoid_gate = jax.nn.sigmoid(gate_proj)
    activated = gate_proj * sigmoid_gate
    hidden = (activated * up_proj).astype(jnp.bfloat16)
    mixed = jnp.dot(hidden, down_weight, preferred_element_type=jnp.float32).astype(jnp.bfloat16)
    hidden_grad = jnp.dot(cotangent, down_weight.T, preferred_element_type=jnp.float32)
    gate_grad = (hidden_grad * up_proj * sigmoid_gate * (1.0 + gate_proj * (1.0 - sigmoid_gate))).astype(jnp.bfloat16)
    up_grad = (hidden_grad * activated).astype(jnp.bfloat16)
    grad_down = jnp.dot(hidden.T, cotangent, preferred_element_type=jnp.float32).astype(jnp.bfloat16)
    grad_gate = jnp.dot(tokens.T, gate_grad, preferred_element_type=jnp.float32).astype(jnp.bfloat16)
    grad_up = jnp.dot(tokens.T, up_grad, preferred_element_type=jnp.float32).astype(jnp.bfloat16)
    token_sum = jnp.dot(gate_grad, gate_weight.T, preferred_element_type=jnp.float32) + jnp.dot(up_grad, up_weight.T, preferred_element_type=jnp.float32)
    grad_tokens = token_sum.astype(jnp.bfloat16)
    return (mixed, grad_tokens, grad_gate, grad_up, grad_down)
```

```python
import jax
import jax.numpy as jnp
from jax import lax
from jax.sharding import PartitionSpec as P

F32 = jnp.float32
BF16 = jnp.bfloat16
F16 = jnp.float16

PROJ_SCALE = 16.0
GRAD_SCALE = 128.0


def dot(left, right, left_dim, right_dim):
    return lax.dot_general(
        left, right, (((left_dim,), (right_dim,)), ((), ())), preferred_element_type=F32
    )


def shift(value, axis, size, by):
    return lax.ppermute(value, axis, [(i, (i + by) % size) for i in range(size)])


def swap_cores(value):
    return lax.ppermute(value, "core", [(0, 1), (1, 0)])


def ring_sum(blocks, depth):
    me = lax.axis_index("col")
    rows = blocks.shape[2] // 2

    def term(offset):
        return lax.dynamic_index_in_dim(blocks, (me + offset) % depth, 0, keepdims=False)

    far = term(depth // 2)
    right = shift(far[:, :rows], "col", depth, 1)
    left = shift(far[:, rows:], "col", depth, -1)
    for hop in range(depth // 2 - 1, 0, -1):
        right, left = lax.optimization_barrier((right, left))
        ahead, behind = term(hop).astype(F32), term(-hop).astype(F32)
        if hop == depth // 2 - 1:
            ahead = jnp.concatenate([ahead[:, :rows] + right.astype(F32), ahead[:, rows:]], axis=1)
            behind = jnp.concatenate([behind[:, :rows], behind[:, rows:] + left.astype(F32)], axis=1)
        else:
            ahead, behind = ahead + right.astype(F32), behind + left.astype(F32)
        ahead, behind = lax.optimization_barrier((ahead.astype(blocks.dtype), behind.astype(blocks.dtype)))
        right, left = shift(ahead, "col", depth, 1), shift(behind, "col", depth, -1)
    return term(0).astype(F32) + right.astype(F32) + left.astype(F32)


def ring_gather(block, depth):
    me = lax.axis_index("col")
    rows = block.shape[1] // 2
    whole = jnp.zeros((block.shape[0], depth) + block.shape[1:], block.dtype)

    def put(whole, part, offset, first=0):
        return lax.dynamic_update_slice(whole, part[:, None], (0, (me + offset) % depth, first, 0))

    whole = put(whole, block, 0)
    right = left = block
    for hop in range(1, depth // 2):
        right, left = shift(right, "col", depth, 1), shift(left, "col", depth, -1)
        whole = put(put(whole, right, -hop), left, hop)
    right = shift(right[:, :rows], "col", depth, 1)
    left = shift(left[:, rows:], "col", depth, -1)
    return put(put(whole, right, depth // 2), left, depth // 2, rows)


def per_device(tokens, cotangent, gate_weight, up_weight, down_weight, *, chips, depth):
    share = tokens.shape[0]
    features, width = gate_weight.shape
    count = 2 * chips * share
    with jax.named_scope("gather_tokens"):
        pair = jnp.concatenate([tokens, cotangent])
        copies = jnp.broadcast_to(pair[None], (chips,) + pair.shape).reshape(count, features)
        mine = lax.all_to_all(copies, ("y", "x"), 0, 0, tiled=True)
        other = swap_cores(mine)
        panel = jnp.stack([mine, other]).reshape(2, chips, 2, share, features)
        panel_tokens = panel[:, :, 0].reshape(count, features)
        panel_cotangent = panel[:, :, 1].reshape(count, features)
    with jax.named_scope("project"):
        terms = [
            (dot(panel_tokens, gate_weight, 1, 0) * PROJ_SCALE).astype(F16),
            (dot(panel_tokens, up_weight, 1, 0) * PROJ_SCALE).astype(F16),
            (dot(panel_cotangent, down_weight, 1, 1) * GRAD_SCALE).astype(F16),
        ]
        blocks = jnp.stack([t.reshape(depth, count // depth, width) for t in terms], axis=1)
    with jax.named_scope("sum_projections"):
        half = blocks.shape[2] // 2
        total = jnp.concatenate(
            [ring_sum(blocks[:, :, :half], depth), ring_sum(blocks[:, :, half:], depth)], axis=1
        )
    with jax.named_scope("gate"):
        gate_proj = total[0] * (1.0 / PROJ_SCALE)
        up_proj = total[1] * (1.0 / PROJ_SCALE)
        hidden_grad = total[2] * (1.0 / GRAD_SCALE)
        sigmoid_gate = jax.nn.sigmoid(gate_proj)
        activated = gate_proj * sigmoid_gate
        hidden = (activated * up_proj).astype(BF16)
        gate_grad = (
            hidden_grad * up_proj * sigmoid_gate * (1.0 + gate_proj * (1.0 - sigmoid_gate))
        ).astype(BF16)
        up_grad = (hidden_grad * activated).astype(BF16)
    with jax.named_scope("gather_hidden"):
        block = jnp.stack([hidden, gate_grad, up_grad])
        half = block.shape[1] // 2
        whole = jnp.concatenate(
            [ring_gather(block[:, :half], depth), ring_gather(block[:, half:], depth)], axis=2
        )
        hidden, gate_grad, up_grad = whole.reshape(3, count, width)
    with jax.named_scope("token_outputs"):
        mixed = dot(hidden, down_weight, 1, 0)
        grad_tokens = dot(gate_grad, gate_weight, 1, 1) + dot(up_grad, up_weight, 1, 1)
        partial = jnp.stack([mixed, grad_tokens]).reshape(2, 2, chips, share, features)
        sent = swap_cores(partial[:, 1].astype(BF16))
    with jax.named_scope("weight_grads"):
        grad_down = dot(hidden, panel_cotangent, 0, 0).astype(BF16)
        grad_gate = dot(panel_tokens, gate_grad, 0, 0).astype(BF16)
        grad_up = dot(panel_tokens, up_grad, 0, 0).astype(BF16)
    with jax.named_scope("scatter_outputs"):
        chip_sum = (partial[:, 0] + sent.astype(F32)).astype(BF16)
        chip_sum = chip_sum.transpose(1, 0, 2, 3).reshape(count, features)
        parts = lax.all_to_all(chip_sum, ("y", "x"), 0, 0, tiled=True)
        out = jnp.sum(parts.reshape(chips, 2, share, features).astype(F32), axis=0).astype(BF16)
    return out[0], out[1], grad_gate, grad_up, grad_down


def solution(mesh):
    row, depth = mesh.devices.shape
    side = 4
    chips = row // 2
    grid = jax.sharding.Mesh(
        mesh.devices.reshape(chips // side, side, 2, depth), ("y", "x", "core", "col")
    )
    rows = ("y", "x", "core")
    tall, wide = P(rows, "col"), P("col", rows)

    def body(*args):
        return per_device(*args, chips=chips, depth=depth)

    return jax.shard_map(
        body,
        mesh=grid,
        in_specs=(tall, tall, wide, wide, tall),
        out_specs=(tall, tall, wide, wide, tall),
        check_vma=False,
    )
```

```python
import jax
import jax.numpy as jnp
from jax import lax
from jax.sharding import PartitionSpec as P

F32 = jnp.float32
BF16 = jnp.bfloat16
F16 = jnp.float16

PROJ_SCALE = 16.0
GRAD_SCALE = 128.0


def dot(left, right, left_dim, right_dim):
    return lax.dot_general(
        left, right, (((left_dim,), (right_dim,)), ((), ())), preferred_element_type=F32
    )


def shift(value, axis, size, by):
    return lax.ppermute(value, axis, [(i, (i + by) % size) for i in range(size)])


def swap_cores(value):
    return lax.ppermute(value, "core", [(0, 1), (1, 0)])


def ring_sum(terms, depth, first, count):
    me = lax.axis_index("col")
    rows = count // 2

    def term(offset):
        spot = ((me + offset) % depth, first, 0)
        shape = (1, count, terms[0].shape[2])
        return jnp.concatenate([lax.dynamic_slice(t, spot, shape) for t in terms]).astype(F32)

    far = term(depth // 2).astype(F16)
    right = shift(far[:, :rows], "col", depth, 1)
    left = shift(far[:, rows:], "col", depth, -1)
    for hop in range(depth // 2 - 1, 0, -1):
        right, left = lax.optimization_barrier((right, left))
        ahead, behind = term(hop), term(-hop)
        if hop == depth // 2 - 1:
            ahead = jnp.concatenate([ahead[:, :rows] + right.astype(F32), ahead[:, rows:]], axis=1)
            behind = jnp.concatenate([behind[:, :rows], behind[:, rows:] + left.astype(F32)], axis=1)
        else:
            ahead, behind = ahead + right.astype(F32), behind + left.astype(F32)
        ahead, behind = lax.optimization_barrier((ahead.astype(F16), behind.astype(F16)))
        right, left = shift(ahead, "col", depth, 1), shift(behind, "col", depth, -1)
    return term(0) + right.astype(F32) + left.astype(F32)


def ring_gather(block, depth):
    me = lax.axis_index("col")
    near = jnp.zeros((block.shape[0], depth) + block.shape[1:], block.dtype)

    def put(near, part, offset):
        return lax.dynamic_update_slice(near, part[:, None], (0, (me + offset) % depth, 0, 0))

    near = put(near, block, 0)
    right = left = block
    for hop in range(1, depth // 2):
        right, left = shift(right, "col", depth, 1), shift(left, "col", depth, -1)
        near = put(put(near, right, -hop), left, hop)
    rows = block.shape[1] // 2
    return near, right[:, :rows], left[:, rows:]


def gates(total):
    gate_proj = total[0] * (1.0 / PROJ_SCALE)
    up_proj = total[1] * (1.0 / PROJ_SCALE)
    hidden_grad = total[2] * (1.0 / GRAD_SCALE)
    sigmoid_gate = jax.nn.sigmoid(gate_proj)
    activated = gate_proj * sigmoid_gate
    hidden = activated * up_proj
    gate_grad = hidden_grad * up_proj * sigmoid_gate * (1.0 + gate_proj * (1.0 - sigmoid_gate))
    up_grad = hidden_grad * activated
    return jnp.stack([hidden, gate_grad, up_grad]).astype(BF16)


def per_device(tokens, cotangent, gate_weight, up_weight, down_weight, *, chips, depth):
    share = tokens.shape[0]
    features, width = gate_weight.shape
    count = 2 * chips * share
    owned = count // depth
    half = owned // 2
    with jax.named_scope("gather_tokens"):
        pair = jnp.concatenate([tokens, cotangent])
        copies = jnp.broadcast_to(pair[None], (chips,) + pair.shape).reshape(count, features)
        mine = lax.all_to_all(copies, ("y", "x"), 0, 0, tiled=True)
        other = swap_cores(mine)

        def split(rows):
            both = rows.reshape(chips, 2, share, features)
            return both[:, 0].reshape(count // 2, features), both[:, 1].reshape(count // 2, features)

        halves = [split(mine), split(other)]
    with jax.named_scope("project"):

        def project(part, weight, dim, scale):
            rows = [(dot(half[part], weight, 1, dim) * scale) for half in halves]
            return jnp.concatenate(rows).reshape(depth, owned, width)

        terms = [
            project(0, gate_weight, 0, PROJ_SCALE),
            project(0, up_weight, 0, PROJ_SCALE),
            project(1, down_weight, 1, GRAD_SCALE),
        ]
        panel_tokens, panel_cotangent = (jnp.concatenate(part) for part in zip(*halves))
    gathered = []
    for first in (0, half):
        with jax.named_scope("sum_projections"):
            total = ring_sum(terms, depth, first, half)
        with jax.named_scope("gate"):
            block = gates(total)
        with jax.named_scope("gather_hidden"):
            gathered.append(ring_gather(block, depth))
    with jax.named_scope("gather_hidden"):
        near, right, left = (jnp.stack(parts, axis=-3) for parts in zip(*gathered))
        near = near.reshape(3, depth, owned, width)
        right, left = lax.optimization_barrier((right, left))
        right, left = shift(right, "col", depth, 1), shift(left, "col", depth, -1)
        far = jnp.concatenate([right, left], axis=2).reshape(3, owned, width)
    with jax.named_scope("token_outputs"):
        spot = (lax.axis_index("col") + depth // 2) % depth

        def outputs(hidden, gate_grad, up_grad):
            mixed = dot(hidden, down_weight, 1, 0)
            return mixed, dot(gate_grad, gate_weight, 1, 1) + dot(up_grad, up_weight, 1, 1)

        early = outputs(*near.reshape(3, count, width))
        late = outputs(*far)
        mixed, grad_tokens = (
            lax.dynamic_update_slice(e.reshape(depth, owned, features), l[None], (spot, 0, 0))
            for e, l in zip(early, late)
        )
        shape = (2, chips, share, features)
        partial = jnp.concatenate([mixed.reshape(shape), grad_tokens.reshape(shape)], axis=2)
        sent = swap_cores(partial[1].astype(BF16))
    with jax.named_scope("weight_grads"):
        whole = lax.dynamic_update_slice(near, far[:, None], (0, spot, 0, 0))
        hidden, gate_grad, up_grad = whole.reshape(3, count, width)
        grad_down = dot(hidden, panel_cotangent, 0, 0).astype(BF16)
        grad_gate = dot(panel_tokens, gate_grad, 0, 0).astype(BF16)
        grad_up = dot(panel_tokens, up_grad, 0, 0).astype(BF16)
    with jax.named_scope("scatter_outputs"):
        chip_sum = (partial[0] + sent.astype(F32)).astype(BF16)
        parts = lax.all_to_all(chip_sum.reshape(count, features), ("y", "x"), 0, 0, tiled=True)
        out = jnp.sum(parts.reshape(chips, 2, share, features).astype(F32), axis=0).astype(BF16)
    return out[0], out[1], grad_gate, grad_up, grad_down


def solution(mesh):
    row, depth = mesh.devices.shape
    side = 4
    chips = row // 2
    grid = jax.sharding.Mesh(
        mesh.devices.reshape(chips // side, side, 2, depth), ("y", "x", "core", "col")
    )
    rows = ("y", "x", "core")
    tall, wide = P(rows, "col"), P("col", rows)

    def body(*args):
        return per_device(*args, chips=chips, depth=depth)

    return jax.shard_map(
        body,
        mesh=grid,
        in_specs=(tall, tall, wide, wide, tall),
        out_specs=(tall, tall, wide, wide, tall),
        check_vma=False,
    )
```

```python
import jax
import jax.numpy as jnp
from jax import lax
from jax.sharding import PartitionSpec as P

F32 = jnp.float32
BF16 = jnp.bfloat16
F16 = jnp.float16

PROJ_SCALE = 2.0**20
GRAD_SCALE = 2.0**23


def dot(left, right, left_dim, right_dim):
    return lax.dot_general(
        left, right, (((left_dim,), (right_dim,)), ((), ())), preferred_element_type=F32
    )


def shift(value, axis, size, by):
    return lax.ppermute(value, axis, [(i, (i + by) % size) for i in range(size)])


def swap_cores(value):
    return lax.ppermute(value, "core", [(0, 1), (1, 0)])


def encode(value):
    root = jnp.sqrt(jnp.abs(value))
    return jnp.where(value < 0, -root, root).astype(F16)


def decode(value):
    value = value.astype(F32)
    return value * jnp.abs(value)


def ring_sum(terms, depth):
    me = lax.axis_index("col")
    rows = terms[0].shape[1] // 2

    def term(offset):
        return jnp.stack([lax.dynamic_index_in_dim(t, (me + offset) % depth, 0, keepdims=False) for t in terms])

    far = encode(term(depth // 2))
    right = shift(far[:, :rows], "col", depth, 1)
    left = shift(far[:, rows:], "col", depth, -1)
    for hop in range(depth // 2 - 1, 0, -1):
        right, left = lax.optimization_barrier((right, left))
        ahead, behind = term(hop), term(-hop)
        if hop == depth // 2 - 1:
            ahead = jnp.concatenate([ahead[:, :rows] + decode(right), ahead[:, rows:]], axis=1)
            behind = jnp.concatenate([behind[:, :rows], behind[:, rows:] + decode(left)], axis=1)
        else:
            ahead, behind = ahead + decode(right), behind + decode(left)
        ahead, behind = lax.optimization_barrier((encode(ahead), encode(behind)))
        right, left = shift(ahead, "col", depth, 1), shift(behind, "col", depth, -1)
    return term(0) + decode(right) + decode(left)


def ring_gather(block, depth):
    me = lax.axis_index("col")
    near = jnp.zeros((block.shape[0], depth) + block.shape[1:], block.dtype)

    def put(near, part, offset):
        return lax.dynamic_update_slice(near, part[:, None], (0, (me + offset) % depth, 0, 0))

    near = put(near, block, 0)
    right = left = block
    for hop in range(1, depth // 2):
        right, left = shift(right, "col", depth, 1), shift(left, "col", depth, -1)
        near = put(put(near, right, -hop), left, hop)
    rows = block.shape[1] // 2
    return near, right[:, :rows], left[:, rows:]


def gates(total):
    gate_proj = total[0] * (1.0 / PROJ_SCALE)
    up_proj = total[1] * (1.0 / PROJ_SCALE)
    hidden_grad = total[2] * (1.0 / GRAD_SCALE)
    sigmoid_gate = jax.nn.sigmoid(gate_proj)
    activated = gate_proj * sigmoid_gate
    hidden = activated * up_proj
    gate_grad = hidden_grad * up_proj * sigmoid_gate * (1.0 + gate_proj * (1.0 - sigmoid_gate))
    up_grad = hidden_grad * activated
    return jnp.stack([hidden, gate_grad, up_grad]).astype(BF16)


def per_device(tokens, cotangent, gate_weight, up_weight, down_weight, *, chips, depth):
    share = tokens.shape[0]
    features, width = gate_weight.shape
    count = 2 * chips * share
    owned = count // 2 // depth
    with jax.named_scope("gather_tokens"):
        pair = jnp.concatenate([tokens, cotangent])
        copies = jnp.broadcast_to(pair[None], (chips,) + pair.shape).reshape(count, features)
        mine = lax.all_to_all(copies, ("y", "x"), 0, 0, tiled=True)
        other = swap_cores(mine)

        def split(rows):
            both = rows.reshape(chips, 2, share, features)
            return both[:, 0].reshape(count // 2, features), both[:, 1].reshape(count // 2, features)

        halves = [split(mine), split(other)]
    gathered = []
    for tokens, cotangent in halves:
        with jax.named_scope("project"):
            grad = dot(cotangent, down_weight, 1, 1) * GRAD_SCALE
            grad, tokens = lax.optimization_barrier((grad, tokens))
            gate = dot(tokens, gate_weight, 1, 0) * PROJ_SCALE
            up = dot(tokens, up_weight, 1, 0) * PROJ_SCALE
            terms = [t.reshape(depth, owned, width) for t in (gate, up, grad)]
        with jax.named_scope("sum_projections"):
            total = ring_sum(terms, depth)
        with jax.named_scope("gate"):
            block = gates(total)
        with jax.named_scope("gather_hidden"):
            gathered.append(ring_gather(block, depth))
    with jax.named_scope("gather_hidden"):
        right, left = (jnp.stack(parts) for parts in list(zip(*gathered))[1:])
        right, left = lax.optimization_barrier((right, left))
        right, left = shift(right, "col", depth, 1), shift(left, "col", depth, -1)
        near = [parts[0] for parts in gathered]
        far = jnp.concatenate([right, left], axis=2)
    with jax.named_scope("token_outputs"):
        spot = (lax.axis_index("col") + depth // 2) % depth

        def outputs(hidden, gate_grad, up_grad):
            mixed = dot(hidden, down_weight, 1, 0)
            return mixed, dot(gate_grad, gate_weight, 1, 1) + dot(up_grad, up_weight, 1, 1)

        def half_outputs(near, far):
            early = outputs(*near.reshape(3, count // 2, width))
            late = outputs(*far)
            both = [
                lax.dynamic_update_slice(e.reshape(depth, owned, features), l[None], (spot, 0, 0))
                for e, l in zip(early, late)
            ]
            return jnp.concatenate([b.reshape(chips, share, features) for b in both], axis=1)

        sent = swap_cores(half_outputs(near[1], far[1]).astype(BF16))
        kept = half_outputs(near[0], far[0])
    with jax.named_scope("weight_grads"):
        panel_tokens, panel_cotangent = (jnp.concatenate(part) for part in zip(*halves))
        whole = [
            lax.dynamic_update_slice(n, f[:, None], (0, spot, 0, 0)).reshape(3, count // 2, width)
            for n, f in zip(near, far)
        ]
        hidden, gate_grad, up_grad = jnp.concatenate(whole, axis=1)
        grad_down = dot(hidden, panel_cotangent, 0, 0).astype(BF16)
        grad_gate = dot(panel_tokens, gate_grad, 0, 0).astype(BF16)
        grad_up = dot(panel_tokens, up_grad, 0, 0).astype(BF16)
    with jax.named_scope("scatter_outputs"):
        chip_sum = (kept + sent.astype(F32)).astype(BF16)
        parts = lax.all_to_all(chip_sum.reshape(count, features), ("y", "x"), 0, 0, tiled=True)
        out = jnp.sum(parts.reshape(chips, 2, share, features).astype(F32), axis=0).astype(BF16)
    return out[0], out[1], grad_gate, grad_up, grad_down


def solution(mesh):
    row, depth = mesh.devices.shape
    side = 4
    chips = row // 2
    grid = jax.sharding.Mesh(
        mesh.devices.reshape(chips // side, side, 2, depth), ("y", "x", "core", "col")
    )
    rows = ("y", "x", "core")
    tall, wide = P(rows, "col"), P("col", rows)

    def body(*args):
        return per_device(*args, chips=chips, depth=depth)

    return jax.shard_map(
        body,
        mesh=grid,
        in_specs=(tall, tall, wide, wide, tall),
        out_specs=(tall, tall, wide, wide, tall),
        check_vma=False,
    )
```

```python
import jax
import jax.numpy as jnp
from jax import lax
from jax.sharding import PartitionSpec as P

F32 = jnp.float32
BF16 = jnp.bfloat16
F16 = jnp.float16

PROJ_SCALE = 2.0**20
GRAD_SCALE = 2.0**23


def dot(left, right, left_dim, right_dim):
    return lax.dot_general(
        left, right, (((left_dim,), (right_dim,)), ((), ())), preferred_element_type=F32
    )


def shift(value, axis, size, by):
    return lax.ppermute(value, axis, [(i, (i + by) % size) for i in range(size)])


def swap_cores(value):
    return lax.ppermute(value, "core", [(0, 1), (1, 0)])


def encode(value):
    return (value * lax.rsqrt(jnp.maximum(jnp.abs(value), 1e-36))).astype(F16)


def decode(value):
    value = value.astype(F32)
    return value * jnp.abs(value)


def ring_sum(terms, depth):
    me = lax.axis_index("col")
    rows = terms[0].shape[1] // 2

    def term(offset):
        return jnp.stack([lax.dynamic_index_in_dim(t, (me + offset) % depth, 0, keepdims=False) for t in terms])

    far = encode(term(depth // 2))
    right = shift(far[:, :rows], "col", depth, 1)
    left = shift(far[:, rows:], "col", depth, -1)
    for hop in range(depth // 2 - 1, 0, -1):
        right, left = lax.optimization_barrier((right, left))
        ahead, behind = term(hop), term(-hop)
        if hop == depth // 2 - 1:
            ahead = jnp.concatenate([ahead[:, :rows] + decode(right), ahead[:, rows:]], axis=1)
            behind = jnp.concatenate([behind[:, :rows], behind[:, rows:] + decode(left)], axis=1)
        else:
            ahead, behind = ahead + decode(right), behind + decode(left)
        ahead, behind = lax.optimization_barrier((encode(ahead), encode(behind)))
        right, left = shift(ahead, "col", depth, 1), shift(behind, "col", depth, -1)
    return term(0) + decode(right) + decode(left)


def ring_gather(block, depth):
    me = lax.axis_index("col")
    near = jnp.zeros((block.shape[0], depth) + block.shape[1:], block.dtype)

    def put(near, part, offset):
        return lax.dynamic_update_slice(near, part[:, None], (0, (me + offset) % depth, 0, 0))

    near = put(near, block, 0)
    right = left = block
    for hop in range(1, depth // 2):
        right, left = shift(right, "col", depth, 1), shift(left, "col", depth, -1)
        near = put(put(near, right, -hop), left, hop)
    rows = block.shape[1] // 2
    return near, right[:, :rows], left[:, rows:]


def gates(total):
    gate_proj = total[0] * (1.0 / PROJ_SCALE)
    up_proj = total[1] * (1.0 / PROJ_SCALE)
    hidden_grad = total[2] * (1.0 / GRAD_SCALE)
    sigmoid_gate = jax.nn.sigmoid(gate_proj)
    activated = gate_proj * sigmoid_gate
    hidden = activated * up_proj
    gate_grad = hidden_grad * up_proj * sigmoid_gate * (1.0 + gate_proj * (1.0 - sigmoid_gate))
    up_grad = hidden_grad * activated
    return jnp.stack([hidden, gate_grad, up_grad]).astype(BF16)


def per_device(tokens, cotangent, gate_weight, up_weight, down_weight, *, chips, depth):
    share = tokens.shape[0]
    features, width = gate_weight.shape
    count = 2 * chips * share
    owned = count // 2 // depth
    with jax.named_scope("gather_tokens"):
        pair = jnp.concatenate([tokens, cotangent])
        copies = jnp.broadcast_to(pair[None], (chips,) + pair.shape).reshape(count, features)
        mine = lax.all_to_all(copies, ("y", "x"), 0, 0, tiled=True)
        other = swap_cores(mine)

        def split(rows):
            both = rows.reshape(chips, 2, share, features)
            return both[:, 0].reshape(count // 2, features), both[:, 1].reshape(count // 2, features)

        halves = [split(mine), split(other)]
    gathered = []
    for tokens, cotangent in halves:
        with jax.named_scope("project"):
            grad = dot(cotangent, down_weight, 1, 1) * GRAD_SCALE
            grad, tokens = lax.optimization_barrier((grad, tokens))
            gate = dot(tokens, gate_weight, 1, 0) * PROJ_SCALE
            up = dot(tokens, up_weight, 1, 0) * PROJ_SCALE
            terms = [t.reshape(depth, owned, width) for t in (gate, up, grad)]
        with jax.named_scope("sum_projections"):
            total = ring_sum(terms, depth)
        with jax.named_scope("gate"):
            block = gates(total)
        with jax.named_scope("gather_hidden"):
            gathered.append(ring_gather(block, depth))
    with jax.named_scope("gather_hidden"):
        right, left = (jnp.stack(parts) for parts in list(zip(*gathered))[1:])
        right, left = lax.optimization_barrier((right, left))
        right, left = shift(right, "col", depth, 1), shift(left, "col", depth, -1)
        near = [parts[0] for parts in gathered]
        far = jnp.concatenate([right, left], axis=2)
    with jax.named_scope("token_outputs"):
        spot = (lax.axis_index("col") + depth // 2) % depth

        def outputs(hidden, gate_grad, up_grad):
            mixed = dot(hidden, down_weight, 1, 0)
            return mixed, dot(gate_grad, gate_weight, 1, 1) + dot(up_grad, up_weight, 1, 1)

        def half_outputs(near, far):
            early = outputs(*near.reshape(3, count // 2, width))
            late = outputs(*far)
            both = [
                lax.dynamic_update_slice(e.reshape(depth, owned, features), l[None], (spot, 0, 0))
                for e, l in zip(early, late)
            ]
            return jnp.concatenate([b.reshape(chips, share, features) for b in both], axis=1)

        sent = swap_cores(half_outputs(near[1], far[1]).astype(BF16))
        kept = half_outputs(near[0], far[0])
    with jax.named_scope("weight_grads"):
        panel_tokens, panel_cotangent = (jnp.concatenate(part) for part in zip(*halves))
        whole = [
            lax.dynamic_update_slice(n, f[:, None], (0, spot, 0, 0)).reshape(3, count // 2, width)
            for n, f in zip(near, far)
        ]
        hidden, gate_grad, up_grad = jnp.concatenate(whole, axis=1)
        grad_down = dot(hidden, panel_cotangent, 0, 0).astype(BF16)
        grad_gate = dot(panel_tokens, gate_grad, 0, 0).astype(BF16)
        grad_up = dot(panel_tokens, up_grad, 0, 0).astype(BF16)
    with jax.named_scope("scatter_outputs"):
        chip_sum = (kept + sent.astype(F32)).astype(BF16)
        parts = lax.all_to_all(chip_sum.reshape(count, features), ("y", "x"), 0, 0, tiled=True)
        out = jnp.sum(parts.reshape(chips, 2, share, features).astype(F32), axis=0).astype(BF16)
    return out[0], out[1], grad_gate, grad_up, grad_down


def solution(mesh):
    row, depth = mesh.devices.shape
    side = 4
    chips = row // 2
    grid = jax.sharding.Mesh(
        mesh.devices.reshape(chips // side, side, 2, depth), ("y", "x", "core", "col")
    )
    rows = ("y", "x", "core")
    tall, wide = P(rows, "col"), P("col", rows)

    def body(*args):
        return per_device(*args, chips=chips, depth=depth)

    return jax.shard_map(
        body,
        mesh=grid,
        in_specs=(tall, tall, wide, wide, tall),
        out_specs=(tall, tall, wide, wide, tall),
        check_vma=False,
    )
```

```python
import jax
import jax.numpy as jnp
from jax import lax
from jax.sharding import PartitionSpec as P

F32 = jnp.float32
BF16 = jnp.bfloat16
F16 = jnp.float16

PROJ_SCALE = 2.0**20
GRAD_SCALE = 2.0**23


def dot(left, right, left_dim, right_dim):
    return lax.dot_general(
        left, right, (((left_dim,), (right_dim,)), ((), ())), preferred_element_type=F32
    )


def shift(value, axis, size, by):
    return lax.ppermute(value, axis, [(i, (i + by) % size) for i in range(size)])


def swap_cores(value):
    return lax.ppermute(value, "core", [(0, 1), (1, 0)])


def encode(value):
    return (value * lax.rsqrt(jnp.maximum(jnp.abs(value), 1e-36))).astype(F16)


def decode(value):
    value = value.astype(F32)
    return value * jnp.abs(value)


def ring_sum(terms, depth):
    me = lax.axis_index("col")
    rows = terms[0].shape[1] // 2

    def term(offset):
        return jnp.stack([lax.dynamic_index_in_dim(t, (me + offset) % depth, 0, keepdims=False) for t in terms])

    far = encode(term(depth // 2))
    right = shift(far[:, :rows], "col", depth, 1)
    left = shift(far[:, rows:], "col", depth, -1)
    for hop in range(depth // 2 - 1, 0, -1):
        right, left = lax.optimization_barrier((right, left))
        ahead, behind = term(hop), term(-hop)
        if hop == depth // 2 - 1:
            ahead = jnp.concatenate([ahead[:, :rows] + decode(right), ahead[:, rows:]], axis=1)
            behind = jnp.concatenate([behind[:, :rows], behind[:, rows:] + decode(left)], axis=1)
        else:
            ahead, behind = ahead + decode(right), behind + decode(left)
        right, left = shift(encode(ahead), "col", depth, 1), shift(encode(behind), "col", depth, -1)
    return term(0) + decode(right) + decode(left)


def ring_gather(block, depth):
    me = lax.axis_index("col")
    near = jnp.zeros((block.shape[0], depth) + block.shape[1:], block.dtype)

    def put(near, part, offset):
        return lax.dynamic_update_slice(near, part[:, None], (0, (me + offset) % depth, 0, 0))

    near = put(near, block, 0)
    right = left = block
    for hop in range(1, depth // 2):
        right, left = shift(right, "col", depth, 1), shift(left, "col", depth, -1)
        near = put(put(near, right, -hop), left, hop)
    rows = block.shape[1] // 2
    return near, right[:, :rows], left[:, rows:]


def gates(total):
    gate_proj = total[0] * (1.0 / PROJ_SCALE)
    up_proj = total[1] * (1.0 / PROJ_SCALE)
    hidden_grad = total[2] * (1.0 / GRAD_SCALE)
    sigmoid_gate = jax.nn.sigmoid(gate_proj)
    activated = gate_proj * sigmoid_gate
    hidden = activated * up_proj
    gate_grad = hidden_grad * up_proj * sigmoid_gate * (1.0 + gate_proj * (1.0 - sigmoid_gate))
    up_grad = hidden_grad * activated
    return jnp.stack([hidden, gate_grad, up_grad]).astype(BF16)


def per_device(tokens, cotangent, gate_weight, up_weight, down_weight, *, chips, depth):
    share = tokens.shape[0]
    features, width = gate_weight.shape
    count = 2 * chips * share
    owned = count // 2 // depth
    with jax.named_scope("gather_tokens"):
        pair = jnp.concatenate([tokens, cotangent])
        copies = jnp.broadcast_to(pair[None], (chips,) + pair.shape).reshape(count, features)
        mine = lax.all_to_all(copies, ("y", "x"), 0, 0, tiled=True)
        other = swap_cores(mine)

        def split(rows):
            both = rows.reshape(chips, 2, share, features)
            return both[:, 0].reshape(count // 2, features), both[:, 1].reshape(count // 2, features)

        halves = [split(mine), split(other)]
    gathered = []
    for tokens, cotangent in halves:
        with jax.named_scope("project"):
            grad = dot(cotangent, down_weight, 1, 1) * GRAD_SCALE
            grad, tokens = lax.optimization_barrier((grad, tokens))
            gate = dot(tokens, gate_weight, 1, 0) * PROJ_SCALE
            up = dot(tokens, up_weight, 1, 0) * PROJ_SCALE
            terms = [t.reshape(depth, owned, width) for t in (gate, up, grad)]
        with jax.named_scope("sum_projections"):
            total = ring_sum(terms, depth)
        with jax.named_scope("gate"):
            block = gates(total)
        with jax.named_scope("gather_hidden"):
            gathered.append(ring_gather(block, depth))
    with jax.named_scope("gather_hidden"):
        right, left = (jnp.stack(parts) for parts in list(zip(*gathered))[1:])
        right, left = lax.optimization_barrier((right, left))
        right, left = shift(right, "col", depth, 1), shift(left, "col", depth, -1)
        near = [parts[0] for parts in gathered]
        far = jnp.concatenate([right, left], axis=2)
    with jax.named_scope("token_outputs"):
        spot = (lax.axis_index("col") + depth // 2) % depth

        def outputs(hidden, gate_grad, up_grad):
            mixed = dot(hidden, down_weight, 1, 0)
            return mixed, dot(gate_grad, gate_weight, 1, 1) + dot(up_grad, up_weight, 1, 1)

        def half_outputs(near, far):
            early = outputs(*near.reshape(3, count // 2, width))
            late = outputs(*far)
            both = [
                lax.dynamic_update_slice(e.reshape(depth, owned, features), l[None], (spot, 0, 0))
                for e, l in zip(early, late)
            ]
            return jnp.concatenate([b.reshape(chips, share, features) for b in both], axis=1)

        sent = swap_cores(half_outputs(near[1], far[1]).astype(BF16))
        kept = half_outputs(near[0], far[0])
    with jax.named_scope("weight_grads"):
        panel_tokens, panel_cotangent = (jnp.concatenate(part) for part in zip(*halves))
        whole = [
            lax.dynamic_update_slice(n, f[:, None], (0, spot, 0, 0)).reshape(3, count // 2, width)
            for n, f in zip(near, far)
        ]
        hidden, gate_grad, up_grad = jnp.concatenate(whole, axis=1)
        grad_down = dot(hidden, panel_cotangent, 0, 0).astype(BF16)
        grad_gate = dot(panel_tokens, gate_grad, 0, 0).astype(BF16)
        grad_up = dot(panel_tokens, up_grad, 0, 0).astype(BF16)
    with jax.named_scope("scatter_outputs"):
        chip_sum = (kept + sent.astype(F32)).astype(BF16)
        parts = lax.all_to_all(chip_sum.reshape(count, features), ("y", "x"), 0, 0, tiled=True)
        out = jnp.sum(parts.reshape(chips, 2, share, features).astype(F32), axis=0).astype(BF16)
    return out[0], out[1], grad_gate, grad_up, grad_down


def solution(mesh):
    row, depth = mesh.devices.shape
    side = 4
    chips = row // 2
    grid = jax.sharding.Mesh(
        mesh.devices.reshape(chips // side, side, 2, depth), ("y", "x", "core", "col")
    )
    rows = ("y", "x", "core")
    tall, wide = P(rows, "col"), P("col", rows)

    def body(*args):
        return per_device(*args, chips=chips, depth=depth)

    return jax.shard_map(
        body,
        mesh=grid,
        in_specs=(tall, tall, wide, wide, tall),
        out_specs=(tall, tall, wide, wide, tall),
        check_vma=False,
    )
```
